512 devices in a mesh: node: 32 (over y, z_lo), local: 16 (over x, z_hi, core).
Axes of the slice: x: 4, y: 4, z: 16 (z_hi: 2, z_lo: 8; z = z_hi * 8 + z_lo), core: 2. Of those that a mesh axis runs over, the one named last changes fastest.
Arguments:
- tokens: bfloat16 [65536, 4096], P(('node', 'local')), may hold values from -24 to 24
- key_codes: bfloat16 [4096, 512], P('local'), may hold values from -0.09375 to 0.09375
- key_exponents: int32 [4096, 2], P('local'), may hold values from -1 to 1
- key_cotangent: bfloat16 [65536, 512], P(('node', 'local')), may hold values from -6 to 6
Outputs:
- keys: bfloat16 [65536, 512], P(('node', 'local'))
- input_grad: bfloat16 [65536, 4096], P(('node', 'local'))
- weight_grad: float32 [4096, 512], P(('node', 'local'))
The draws below stay inside these ranges and needn't reach their ends.
Inputs may be any that keep to these rules, and one draw needn't show every extreme that they name: key_exponents gives the power of two that scales each block of 256 columns of a row of key_codes.
All inputs are finite; a program needn't handle non-finite values.
Results may differ from the reference program's by a relative error of at most 0.015.
Values may be sent and summed in bfloat16 or wider, within the bound.
No kernel may reach another device: no remote copies, remote signals or barrier semaphores. Data moves between devices by JAX's collectives and lax.ppermute only.
A program may use at most 128 MiB of HBM per device.

```python
import math
import jax
import jax.numpy as jnp
from jax import lax

DW = 4096
KVH = 4
HEAD = 128
QBLOCK = 256
SEQ = 8192
TOK_DEV = 128
KV = 512
TOKENS = 65536
N_NODE = 32
N_LOCAL = 16


def touch_ends(array, rng, smallest, high):
    longest = array.shape.index(max(array.shape))
    spots = []
    for shift in (0, 1):
        where = [jax.random.randint(jax.random.fold_in(rng, axis), (), 0, length) for axis, length in enumerate(array.shape)]
        where[longest] = (where[longest] + shift) % array.shape[longest]
        spots.append(tuple(where))
    return array.at[spots[0]].set(smallest).at[spots[1]].set(high)


def with_spikes(values, key, source, target, parts, factor):
    owner, partner = [(jnp.arange(values.shape[position]) // (values.shape[position] // parts)).reshape([-1 if axis == position else 1 for axis in range(values.ndim)]) for position in (source, target)]
    chosen = jax.random.permutation(key, parts)[partner]
    strong = (owner == chosen) | (owner == (partner + parts // 2) % parts)
    return jnp.where(strong, factor * values, values)


def block_levels(own_key, dims, split, least, high):
    gain = 1.0
    for axis_at, shards_of in split:
        draws = jax.random.uniform(jax.random.fold_in(jax.random.fold_in(own_key, 6), axis_at), (shards_of,), jnp.float32, least / len(split), high / len(split))
        gain = gain * jnp.repeat(jnp.exp(draws), dims[axis_at] // shards_of).reshape((-1,) + (1,) * (len(dims) - 1 - axis_at))
    return gain


def normal_values(stream_key, extent, spread, reach, cuts=(), kind=jnp.bfloat16):
    entries = spread * jax.random.normal(stream_key, extent, jnp.float32)
    if cuts:
        entries = entries * block_levels(stream_key, extent, cuts, -0.22, 0.18)
    return jnp.clip(entries, -reach, reach).astype(kind)


def bell_draw_with(stream_key, extent, deviation, limit, shards, heavy, held_as=jnp.bfloat16):
    entries = deviation * jax.random.normal(stream_key, extent, jnp.float32)
    if shards:
        entries = entries * block_levels(stream_key, extent, shards, -0.22, 0.18)
    return jnp.clip(with_spikes(entries, jax.random.fold_in(stream_key, 3), *heavy), -limit, limit).astype(held_as)


def setup_inputs(seed: int = 0) -> dict:
    streams_of = jax.random.split(jax.random.key(seed), 5)
    return {
        "tokens": bell_draw_with(streams_of[0], (TOKENS, DW), 1.0, 24.0, ((0, 512),), (0, 1, 512, 6.0)),
        "key_codes": normal_values(streams_of[1], (DW, KV), DW ** -0.5, 0.09375, ((0, 16),)),
        "key_exponents": touch_ends(jax.random.randint(streams_of[2], (DW, KV // QBLOCK), -1, 2), jax.random.fold_in(streams_of[2], 1), -1, 1).astype(jnp.int32),
        "key_cotangent": normal_values(streams_of[3], (TOKENS, KV), 1.0, 6.0, ((0, 512),)),
    }


THETA = 500000.0

def tables(positions):
    inverse = THETA ** (-(jnp.arange(HEAD // 2, dtype=jnp.float32) * 2.0 / HEAD))
    angles = positions.astype(jnp.float32)[:, None] * inverse[None, :]
    return (jnp.cos(angles), jnp.sin(angles))

def rotate(values, cosine, sine_part):
    count = values.shape[0]
    heads = values.reshape(count, KVH, HEAD)
    first_half = heads[:, :, :HEAD // 2]
    second_half = heads[:, :, HEAD // 2:]
    cos_rows = cosine[:, None, :]
    sin_rows = sine_part[:, None, :]
    joined = jnp.concatenate([first_half * cos_rows - second_half * sin_rows, second_half * cos_rows + first_half * sin_rows], axis=2)
    return joined.reshape(count, KVH * HEAD)

def unrotate(values, cosine, sine_part):
    count = values.shape[0]
    heads = values.reshape(count, KVH, HEAD)
    first_half = heads[:, :, :HEAD // 2]
    second_half = heads[:, :, HEAD // 2:]
    cos_rows = cosine[:, None, :]
    sin_rows = sine_part[:, None, :]
    joined = jnp.concatenate([first_half * cos_rows + second_half * sin_rows, second_half * cos_rows - first_half * sin_rows], axis=2)
    return joined.reshape(count, KVH * HEAD)

def quantize(partial_value):
    blocks = partial_value.reshape(partial_value.shape[0], partial_value.shape[1] // QBLOCK, QBLOCK)
    largest = lax.optimization_barrier(jnp.max(jnp.abs(blocks), axis=2))
    block_scale = jnp.exp2(jnp.ceil(jnp.log2(largest + 1e-06)))
    code_values = (blocks / block_scale[:, :, None]).astype(jnp.bfloat16)
    return (code_values, block_scale.astype(jnp.bfloat16))

def dequantize(code_values, block_scale):
    values = code_values.astype(jnp.float32) * block_scale.astype(jnp.float32)[..., None]
    return values.reshape(values.shape[0], values.shape[1] * values.shape[2])

def reference(tokens, key_codes, key_exponents, key_cotangent):
    expanded = jnp.repeat(jnp.exp2(key_exponents.astype(jnp.float32)), QBLOCK, axis=1)
    weights = (key_codes.astype(jnp.float32) * expanded).astype(jnp.bfloat16)
    positions = jnp.arange(TOKENS, dtype=jnp.int32) % SEQ
    cosine, sine_part = tables(positions)
    projected = jnp.dot(tokens, weights, preferred_element_type=jnp.float32)
    keys = rotate(projected, cosine, sine_part).astype(jnp.bfloat16)
    pre_grad = unrotate(key_cotangent.astype(jnp.float32), cosine, sine_part).astype(jnp.bfloat16)
    input_grad = lax.dot_general(pre_grad, weights, (((1,), (1,)), ((), ())), preferred_element_type=jnp.float32).astype(jnp.bfloat16)
    device_count = N_NODE * N_LOCAL

    def accumulate(summed, device_block):
        block_rows, grad_rows = device_block
        partial_value = lax.dot_general(block_rows, grad_rows, (((0,), (0,)), ((), ())), preferred_element_type=jnp.float32)
        code_values, block_scale = quantize(partial_value)
        return (summed + dequantize(code_values, block_scale), None)
    summed, _ = lax.scan(accumulate, jnp.zeros((DW, KV), jnp.float32), (tokens.reshape(device_count, TOK_DEV, DW), pre_grad.reshape(device_count, TOK_DEV, KV)))
    weight_grad = summed * (1.0 / math.sqrt(TOKENS))
    return (keys, input_grad, weight_grad)
```

```python
import math

import jax
import jax.numpy as jnp
from jax import lax
from jax.experimental import pallas as pl
from jax.experimental.pallas import tpu as pltpu
from jax.sharding import Mesh
from jax.sharding import PartitionSpec as P

KVH = 4
HEAD = 128
QBLOCK = 256
SEQ = 8192
THETA = 500000.0

Y, ZL, X, ZH, CORE = 4, 8, 4, 2, 2
AXES = ("y", "zl", "x", "zh", "core")
ROW = 8

F32 = jnp.float32
BF16 = jnp.bfloat16
PARAMS = pltpu.CompilerParams(vmem_limit_bytes=32 * 1024 * 1024)


def dequantize_kernel(code_ref, exponent_ref, weight_ref):
    scale = jnp.exp2(exponent_ref[...].astype(F32))
    for block in range(code_ref.shape[1] // QBLOCK):
        columns = slice(block * QBLOCK, (block + 1) * QBLOCK)
        value = code_ref[:, columns].astype(F32) * scale[:, block : block + 1]
        weight_ref[:, columns] = value.astype(BF16)


def dequantize(key_codes, key_exponents):
    return pl.pallas_call(
        dequantize_kernel,
        out_shape=jax.ShapeDtypeStruct(key_codes.shape, BF16),
        compiler_params=PARAMS,
    )(key_codes, key_exponents)


def tables(positions):
    inverse = THETA ** (-(jnp.arange(HEAD // 2, dtype=F32) * 2.0 / HEAD))
    angles = positions.astype(F32)[:, None] * inverse[None, :]
    cosine, sine = jnp.cos(angles), jnp.sin(angles)
    return (
        jnp.concatenate([cosine, cosine], axis=1),
        jnp.concatenate([-sine, sine], axis=1),
    )


def partial_kernel(core_ref, token_ref, cot_ref, cos_ref, sin_ref, mine_ref, theirs_ref, pre_ref, part_ref):
    @pl.when(pl.program_id(0) == 0)
    def _():
        for head in range(KVH):
            columns = slice(head * HEAD, (head + 1) * HEAD)
            value = cot_ref[:, columns].astype(F32)
            turned = pltpu.roll(value, HEAD // 2, 1)
            pre_ref[:, columns] = (value * cos_ref[...] - turned * sin_ref[...]).astype(BF16)

    part = lax.dot_general(
        token_ref[...], pre_ref[...], (((0,), (0,)), ((), ())), preferred_element_type=F32
    )
    part_ref[...] = part.reshape(part_ref.shape)
    core = core_ref[0]
    for x in range(X):
        for zl in range(ZL):
            for zh in range(ZH):
                place = (zl * X + x) * ZH + zh
                mine_ref[x, 0, zl, zh] = part_ref[place, core].astype(BF16)
                theirs_ref[x, 0, zl, zh] = part_ref[place, 1 - core].astype(BF16)


def partial_products(core, tokens, key_cotangent, cosine, sine):
    count, width = tokens.shape
    features = key_cotangent.shape[1]
    step = width // Y
    half = jax.ShapeDtypeStruct((X, Y, ZL, ZH, ROW, features), BF16)
    half_spec = pl.BlockSpec((X, 1, ZL, ZH, ROW, features), lambda y: (0, y, 0, 0, 0, 0))
    whole = lambda y: (0, 0)
    return pl.pallas_call(
        partial_kernel,
        grid=(Y,),
        in_specs=[
            pl.BlockSpec(memory_space=pltpu.SMEM),
            pl.BlockSpec((count, step), lambda y: (0, y)),
            pl.BlockSpec((count, features), whole),
            pl.BlockSpec((count, HEAD), whole),
            pl.BlockSpec((count, HEAD), whole),
        ],
        out_specs=[half_spec, half_spec, pl.BlockSpec((count, features), whole)],
        out_shape=[half, half, jax.ShapeDtypeStruct((count, features), BF16)],
        scratch_shapes=[pltpu.VMEM((ZL * X * ZH, CORE, ROW, features), F32)],
        compiler_params=PARAMS,
    )(core, tokens, key_cotangent, cosine, sine)


def apply_kernel(place_ref, token_ref, pre_ref, cos_ref, sin_ref, w00_ref, w01_ref, w10_ref, w11_ref, keys_ref, grad_ref):
    zh, core = place_ref[0], place_ref[1]
    rows = token_ref.shape[1] // (X * ZH * CORE)
    pre = pre_ref[...]
    total = jnp.zeros(pre.shape, F32)
    held = ((w00_ref, 0, 0), (w01_ref, 0, 1), (w10_ref, 1, 0), (w11_ref, 1, 1))
    for weight_ref, other_zh, other_core in held:
        near = jnp.where(other_zh == 0, zh, 1 - zh)
        side = jnp.where(other_core == 0, core, 1 - core)
        for x in range(X):
            start = pl.multiple_of(((x * ZH + near) * CORE + side) * rows, rows)
            weight = weight_ref[x * rows : (x + 1) * rows, :]
            total += jnp.dot(token_ref[:, pl.ds(start, rows)], weight, preferred_element_type=F32)
            grad_ref[:, pl.ds(start, rows)] = lax.dot_general(
                pre, weight, (((1,), (1,)), ((), ())), preferred_element_type=F32
            ).astype(BF16)
    for head in range(KVH):
        columns = slice(head * HEAD, (head + 1) * HEAD)
        value = total[:, columns]
        turned = pltpu.roll(value, HEAD // 2, 1)
        keys_ref[:, columns] = (value * cos_ref[...] + turned * sin_ref[...]).astype(BF16)


def apply_weights(place, tokens, pre_grad, cosine, sine, weights):
    vmem = pl.BlockSpec(memory_space=pltpu.VMEM)
    return pl.pallas_call(
        apply_kernel,
        in_specs=[pl.BlockSpec(memory_space=pltpu.SMEM)] + [vmem] * 8,
        out_specs=[vmem, vmem],
        out_shape=[
            jax.ShapeDtypeStruct(pre_grad.shape, BF16),
            jax.ShapeDtypeStruct(tokens.shape, BF16),
        ],
        compiler_params=PARAMS,
        cost_estimate=pl.CostEstimate(
            flops=4 * tokens.shape[0] * tokens.shape[1] * pre_grad.shape[1],
            bytes_accessed=7 * 1024 * 1024,
            transcendentals=0,
        ),
    )(place, tokens, pre_grad, cosine, sine, *weights)


def swap(value, axis):
    return lax.ppermute(value, axis, [(0, 1), (1, 0)])


def on_device(tokens, key_codes, key_exponents, key_cotangent):
    y, zl, x, zh, core = [lax.axis_index(name) for name in AXES]
    count = tokens.shape[0]
    features = key_cotangent.shape[1]

    shard = dequantize(key_codes, key_exponents)
    near = lax.all_gather(shard, "x", axis=0, tiled=True)
    far = lax.all_gather(swap(shard, "zh"), "x", axis=0, tiled=True)
    weights = (near, swap(near, "core"), far, swap(far, "core"))

    device_index = (((y * ZL + zl) * X + x) * ZH + zh) * CORE + core
    positions = (device_index * count + jnp.arange(count, dtype=jnp.int32)) % SEQ
    cosine, sine = tables(positions)
    mine, theirs, pre_grad = partial_products(core[None], tokens, key_cotangent, cosine, sine)

    summed = (mine.astype(F32) + swap(theirs, "core").astype(F32)).astype(BF16)
    summed = summed.reshape(X * Y, ZL * ZH, ROW, features)
    got = lax.all_to_all(summed, ("x", "y"), split_axis=0, concat_axis=0, tiled=True)
    summed = jnp.sum(got.astype(F32), axis=0).astype(BF16)
    got = lax.all_to_all(summed, ("zl", "zh"), split_axis=0, concat_axis=0, tiled=True)
    total_tokens = count * Y * ZL * X * ZH * CORE
    weight_grad = jnp.sum(got.astype(F32), axis=0) * (1.0 / math.sqrt(total_tokens))

    place = jnp.stack([zh, core])
    keys, input_grad = apply_weights(place, tokens, pre_grad, cosine, sine, weights)
    return keys, input_grad, weight_grad


def solution(mesh):
    fine = Mesh(mesh.devices.reshape(Y, ZL, X, ZH, CORE), AXES)
    split = P(AXES, None)
    return jax.shard_map(
        on_device,
        mesh=fine,
        in_specs=(split, P(("x", "zh", "core"), None), P(("x", "zh", "core"), None), split),
        out_specs=(split, split, split),
        check_vma=False,
    )
```

```python
import math

import jax
import jax.numpy as jnp
from jax import lax
from jax.experimental import pallas as pl
from jax.experimental.pallas import tpu as pltpu
from jax.sharding import Mesh
from jax.sharding import PartitionSpec as P

KVH = 4
HEAD = 128
QBLOCK = 256
SEQ = 8192
THETA = 500000.0

Y, ZL, X, ZH, CORE = 4, 8, 4, 2, 2
AXES = ("y", "zl", "x", "zh", "core")
ROW = 8

F32 = jnp.float32
BF16 = jnp.bfloat16
PARAMS = pltpu.CompilerParams(vmem_limit_bytes=20 * 1024 * 1024)


def dequantize_kernel(code_ref, exponent_ref, weight_ref):
    scale = jnp.exp2(exponent_ref[...].astype(F32))
    for block in range(code_ref.shape[1] // QBLOCK):
        columns = slice(block * QBLOCK, (block + 1) * QBLOCK)
        value = code_ref[:, columns].astype(F32) * scale[:, block : block + 1]
        weight_ref[:, columns] = value.astype(BF16)


def dequantize(key_codes, key_exponents):
    return pl.pallas_call(
        dequantize_kernel,
        out_shape=jax.ShapeDtypeStruct(key_codes.shape, BF16),
        compiler_params=PARAMS,
    )(key_codes, key_exponents)


def tables(positions):
    inverse = THETA ** (-(jnp.arange(HEAD // 2, dtype=F32) * 2.0 / HEAD))
    angles = positions.astype(F32)[:, None] * inverse[None, :]
    cosine, sine = jnp.cos(angles), jnp.sin(angles)
    return (
        jnp.concatenate([cosine, cosine], axis=1),
        jnp.concatenate([-sine, sine], axis=1),
    )


def partial_kernel(core_ref, token_ref, cot_ref, cos_ref, sin_ref, mine_ref, theirs_ref, pre_ref, part_ref):
    @pl.when(pl.program_id(0) == 0)
    def _():
        for head in range(KVH):
            columns = slice(head * HEAD, (head + 1) * HEAD)
            value = cot_ref[:, columns].astype(F32)
            turned = pltpu.roll(value, HEAD // 2, 1)
            pre_ref[:, columns] = (value * cos_ref[...] - turned * sin_ref[...]).astype(BF16)

    part = lax.dot_general(
        token_ref[...], pre_ref[...], (((0,), (0,)), ((), ())), preferred_element_type=F32
    )
    part_ref[...] = part.reshape(part_ref.shape)
    core = core_ref[0]
    for x in range(X):
        for zl in range(ZL):
            for zh in range(ZH):
                place = (zl * X + x) * ZH + zh
                mine_ref[x, 0, zl, zh] = part_ref[place, core].astype(BF16)
                theirs_ref[x, 0, zl, zh] = part_ref[place, 1 - core].astype(BF16)


def partial_products(core, tokens, key_cotangent, cosine, sine):
    count, width = tokens.shape
    features = key_cotangent.shape[1]
    step = width // Y
    half = jax.ShapeDtypeStruct((X, Y, ZL, ZH, ROW, features), BF16)
    half_spec = pl.BlockSpec((X, 1, ZL, ZH, ROW, features), lambda y: (0, y, 0, 0, 0, 0))
    whole = lambda y: (0, 0)
    return pl.pallas_call(
        partial_kernel,
        grid=(Y,),
        in_specs=[
            pl.BlockSpec(memory_space=pltpu.SMEM),
            pl.BlockSpec((count, step), lambda y: (0, y)),
            pl.BlockSpec((count, features), whole),
            pl.BlockSpec((count, HEAD), whole),
            pl.BlockSpec((count, HEAD), whole),
        ],
        out_specs=[half_spec, half_spec, pl.BlockSpec((count, features), whole)],
        out_shape=[half, half, jax.ShapeDtypeStruct((count, features), BF16)],
        scratch_shapes=[pltpu.VMEM((ZL * X * ZH, CORE, ROW, features), F32)],
        compiler_params=PARAMS,
    )(core, tokens, key_cotangent, cosine, sine)


def join_kernel(*refs):
    rows = refs[0].shape[0]
    for block, ref in enumerate(refs[:-1]):
        refs[-1][block * rows : (block + 1) * rows, :] = ref[...]


def joined(blocks):
    rows, features = blocks[0].shape
    return pl.pallas_call(
        join_kernel,
        out_shape=jax.ShapeDtypeStruct((len(blocks) * rows, features), BF16),
        compiler_params=PARAMS,
    )(*blocks)


def first_column(place_ref, block, side, rows):
    x, zh = place_ref[0], place_ref[1]
    near = zh if block < X else 1 - zh
    source = lax.rem(x + (X - block % X), X)
    return pl.multiple_of(((source * ZH + near) * CORE + side) * rows, rows)


def apply_first_kernel(place_ref, token_ref, pre_ref, weight_ref, total_ref, grad_ref):
    rows = weight_ref.shape[0] // (ZH * X)
    pre = pre_ref[...]
    total = jnp.zeros(pre.shape, F32)
    for block in range(ZH * X):
        start = first_column(place_ref, block, place_ref[2], rows)
        weight = weight_ref[block * rows : (block + 1) * rows, :]
        total += jnp.dot(token_ref[:, pl.ds(start, rows)], weight, preferred_element_type=F32)
        grad_ref[block] = lax.dot_general(
            pre, weight, (((1,), (1,)), ((), ())), preferred_element_type=F32
        ).astype(BF16)
    total_ref[...] = total


def apply_second_kernel(place_ref, token_ref, pre_ref, cos_ref, sin_ref, weight_ref, total_ref, half_ref, keys_ref, grad_ref):
    rows = weight_ref.shape[0] // (ZH * X)
    pre = pre_ref[...]
    total = total_ref[...]
    for block in range(ZH * X):
        start = first_column(place_ref, block, place_ref[2], rows)
        grad_ref[:, pl.ds(start, rows)] = half_ref[block]
        start = first_column(place_ref, block, 1 - place_ref[2], rows)
        weight = weight_ref[block * rows : (block + 1) * rows, :]
        total += jnp.dot(token_ref[:, pl.ds(start, rows)], weight, preferred_element_type=F32)
        grad_ref[:, pl.ds(start, rows)] = lax.dot_general(
            pre, weight, (((1,), (1,)), ((), ())), preferred_element_type=F32
        ).astype(BF16)
    for head in range(KVH):
        columns = slice(head * HEAD, (head + 1) * HEAD)
        value = total[:, columns]
        turned = pltpu.roll(value, HEAD // 2, 1)
        keys_ref[:, columns] = (value * cos_ref[...] + turned * sin_ref[...]).astype(BF16)


def product_cost(tokens, features):
    return pl.CostEstimate(
        flops=2 * tokens.shape[0] * tokens.shape[1] * features,
        bytes_accessed=4 * 1024 * 1024,
        transcendentals=0,
    )


def apply_first(place, tokens, pre_grad, weights):
    vmem = pl.BlockSpec(memory_space=pltpu.VMEM)
    count, features = pre_grad.shape
    blocks = ZH * X
    return pl.pallas_call(
        apply_first_kernel,
        in_specs=[pl.BlockSpec(memory_space=pltpu.SMEM)] + [vmem] * 3,
        out_specs=[vmem, vmem],
        out_shape=[
            jax.ShapeDtypeStruct((count, features), F32),
            jax.ShapeDtypeStruct((blocks, count, weights.shape[0] // blocks), BF16),
        ],
        compiler_params=PARAMS,
        cost_estimate=product_cost(tokens, features),
    )(place, tokens, pre_grad, weights)


def apply_second(place, tokens, pre_grad, cosine, sine, weights, total, half):
    vmem = pl.BlockSpec(memory_space=pltpu.VMEM)
    return pl.pallas_call(
        apply_second_kernel,
        in_specs=[pl.BlockSpec(memory_space=pltpu.SMEM)] + [vmem] * 7,
        out_specs=[vmem, vmem],
        out_shape=[
            jax.ShapeDtypeStruct(pre_grad.shape, BF16),
            jax.ShapeDtypeStruct(tokens.shape, BF16),
        ],
        compiler_params=PARAMS,
        cost_estimate=product_cost(tokens, pre_grad.shape[1]),
    )(place, tokens, pre_grad, cosine, sine, weights, total, half)


def after(value, *others):
    return lax.optimization_barrier((value, *others))[0]


def from_x(shard):
    moved = [lax.ppermute(shard, "x", [(i, (i + k) % X) for i in range(X)]) for k in range(1, X)]
    return [shard, *moved]


def swap(value, axis):
    return lax.ppermute(value, axis, [(0, 1), (1, 0)])


def on_device(tokens, key_codes, key_exponents, key_cotangent):
    y, zl, x, zh, core = [lax.axis_index(name) for name in AXES]
    count = tokens.shape[0]
    features = key_cotangent.shape[1]

    shard = dequantize(key_codes, key_exponents)
    device_index = (((y * ZL + zl) * X + x) * ZH + zh) * CORE + core
    positions = (device_index * count + jnp.arange(count, dtype=jnp.int32)) % SEQ
    cosine, sine = tables(positions)
    mine, theirs, pre_grad = partial_products(core[None], after(tokens, shard), key_cotangent, cosine, sine)

    summed = (mine.astype(F32) + swap(theirs, "core").astype(F32)).astype(BF16)
    summed = summed.reshape(X * Y, ZL * ZH, ROW, features)
    got = lax.all_to_all(summed, ("x", "y"), split_axis=0, concat_axis=0, tiled=True)

    shard = after(shard, theirs)
    far_shard = after(swap(shard, "zh"), summed)
    near = from_x(shard)
    far = from_x(far_shard)

    held = joined(near + far)
    got = after(got, held)
    summed = jnp.sum(got.astype(F32), axis=0).astype(BF16)
    got = lax.all_to_all(summed, ("zl", "zh"), split_axis=0, concat_axis=0, tiled=True)

    place = jnp.stack([x, zh, core])
    total, half = apply_first(place, tokens, pre_grad, held)
    keys, input_grad = apply_second(
        place, tokens, pre_grad, cosine, sine, swap(held, "core"), total, half
    )
    got = after(got, keys)
    total_tokens = count * Y * ZL * X * ZH * CORE
    weight_grad = jnp.sum(got.astype(F32), axis=0) * (1.0 / math.sqrt(total_tokens))
    return keys, input_grad, weight_grad


def solution(mesh):
    fine = Mesh(mesh.devices.reshape(Y, ZL, X, ZH, CORE), AXES)
    split = P(AXES, None)
    return jax.shard_map(
        on_device,
        mesh=fine,
        in_specs=(split, P(("x", "zh", "core"), None), P(("x", "zh", "core"), None), split),
        out_specs=(split, split, split),
        check_vma=False,
    )
```

```python
import math

import jax
import jax.numpy as jnp
from jax import lax
from jax.experimental import pallas as pl
from jax.experimental.pallas import tpu as pltpu
from jax.sharding import Mesh
from jax.sharding import PartitionSpec as P

KVH = 4
HEAD = 128
QBLOCK = 256
SEQ = 8192
THETA = 500000.0

Y, ZL, X, ZH, CORE = 4, 8, 4, 2, 2
AXES = ("y", "zl", "x", "zh", "core")
ROW = 8

F32 = jnp.float32
BF16 = jnp.bfloat16
PARAMS = pltpu.CompilerParams(vmem_limit_bytes=20 * 1024 * 1024)
SMEM = pl.BlockSpec(memory_space=pltpu.SMEM)
VMEM = pl.BlockSpec(memory_space=pltpu.VMEM)


def dequantize_kernel(code_ref, exponent_ref, weight_ref):
    scale = jnp.exp2(exponent_ref[...].astype(F32))
    for block in range(code_ref.shape[1] // QBLOCK):
        columns = slice(block * QBLOCK, (block + 1) * QBLOCK)
        value = code_ref[:, columns].astype(F32) * scale[:, block : block + 1]
        weight_ref[:, columns] = value.astype(BF16)


def dequantize(key_codes, key_exponents):
    return pl.pallas_call(
        dequantize_kernel,
        out_shape=jax.ShapeDtypeStruct(key_codes.shape, BF16),
        compiler_params=PARAMS,
    )(key_codes, key_exponents)


def tables(positions):
    inverse = THETA ** (-(jnp.arange(HEAD // 2, dtype=F32) * 2.0 / HEAD))
    angles = positions.astype(F32)[:, None] * inverse[None, :]
    cosine, sine = jnp.cos(angles), jnp.sin(angles)
    return (
        jnp.concatenate([cosine, cosine], axis=1),
        jnp.concatenate([-sine, sine], axis=1),
    )


def pack_kernel(token_ref, cot_ref, cos_ref, sin_ref, packed_ref, pre_ref):
    width = token_ref.shape[1]

    @pl.when(pl.program_id(0) == 0)
    def _():
        for head in range(KVH):
            columns = slice(head * HEAD, (head + 1) * HEAD)
            value = cot_ref[:, columns].astype(F32)
            turned = pltpu.roll(value, HEAD // 2, 1)
            pre_ref[:, columns] = (value * cos_ref[...] - turned * sin_ref[...]).astype(BF16)

    packed_ref[0, :, :width] = token_ref[...]
    packed_ref[0, :, width:] = pre_ref[...]


def packed_for_y(tokens, key_cotangent, cosine, sine):
    count, width = tokens.shape
    features = key_cotangent.shape[1]
    whole = lambda y: (0, 0)
    return pl.pallas_call(
        pack_kernel,
        grid=(Y,),
        in_specs=[
            pl.BlockSpec((count, width // Y), lambda y: (0, y)),
            pl.BlockSpec((count, features), whole),
            pl.BlockSpec((count, HEAD), whole),
            pl.BlockSpec((count, HEAD), whole),
        ],
        out_specs=pl.BlockSpec((1, count, width // Y + features), lambda y: (y, 0, 0)),
        out_shape=jax.ShapeDtypeStruct((Y, count, width // Y + features), BF16),
        scratch_shapes=[pltpu.VMEM((count, features), BF16)],
        compiler_params=PARAMS,
    )(tokens, key_cotangent, cosine, sine)


def partial_kernel(token_ref, pre_ref, part_ref):
    rows = token_ref.shape[0] * token_ref.shape[1]
    part = lax.dot_general(
        token_ref[...].reshape(rows, token_ref.shape[2]),
        pre_ref[...].reshape(rows, pre_ref.shape[2]),
        (((0,), (0,)), ((), ())),
        preferred_element_type=F32,
    )
    part = part.reshape(-1, ROW, part.shape[1])
    for zl in range(part_ref.shape[2]):
        for x in range(X):
            for zh in range(ZH):
                for core in range(CORE):
                    place = ((zl * X + x) * ZH + zh) * CORE + core
                    part_ref[x, core, zl, zh] = part[place].astype(BF16)


def partial_products(got, features):
    count = got.shape[1]
    width = got.shape[2] - features
    steps = 4
    return pl.pallas_call(
        partial_kernel,
        grid=(steps,),
        in_specs=[
            pl.BlockSpec((Y, count, width // steps), lambda i: (0, 0, i)),
            pl.BlockSpec((Y, count, features), lambda i: (0, 0, width // features)),
        ],
        out_specs=pl.BlockSpec(
            (X, CORE, ZL // steps, ZH, ROW, features), lambda i: (0, 0, i, 0, 0, 0)
        ),
        out_shape=jax.ShapeDtypeStruct((X, CORE, ZL, ZH, ROW, features), BF16),
        compiler_params=PARAMS,
    )(got, got)


def apply_kernel(place_ref, got_ref, w00_ref, w01_ref, w10_ref, w11_ref, *out_refs):
    y, zh, core = place_ref[0], place_ref[1], place_ref[2]
    rows, features = w00_ref.shape
    width = ZH * CORE * rows
    held = ((w00_ref, zh, core), (w01_ref, zh, 1 - core), (w10_ref, 1 - zh, core), (w11_ref, 1 - zh, 1 - core))
    for ahead, out_ref in enumerate(out_refs):
        target = lax.rem(y + ahead, Y)
        pre = got_ref[target, :, width:]
        total = jnp.zeros(pre.shape, F32)
        for weight_ref, near, side in held:
            start = pl.multiple_of((near * CORE + side) * rows, rows)
            weight = weight_ref[...]
            total += jnp.dot(
                got_ref[target, :, pl.ds(start, rows)], weight, preferred_element_type=F32
            )
            out_ref[:, pl.ds(start, rows)] = lax.dot_general(
                pre, weight, (((1,), (1,)), ((), ())), preferred_element_type=F32
            ).astype(BF16)
        out_ref[:, width:] = total.astype(BF16)


def apply_weights(place, got, weights):
    count = got.shape[1]
    one = jax.ShapeDtypeStruct((count, got.shape[2]), BF16)
    return pl.pallas_call(
        apply_kernel,
        in_specs=[SMEM] + [VMEM] * 5,
        out_specs=[VMEM] * Y,
        out_shape=[one] * Y,
        compiler_params=PARAMS,
        cost_estimate=pl.CostEstimate(
            flops=2 * 2 * count * Y * got.shape[2] * 512,
            bytes_accessed=6 * 1024 * 1024,
            transcendentals=0,
        ),
    )(place, got, *weights)


def finish_kernel(place_ref, cos_ref, sin_ref, *refs):
    got_refs, keys_ref, grad_ref = refs[:Y], refs[Y], refs[Y + 1]
    width = grad_ref.shape[1] // Y
    for behind, got_ref in enumerate(got_refs):
        source = lax.rem(place_ref[0] + (Y - behind), Y)
        start = pl.multiple_of(source * width, width)
        grad_ref[:, pl.ds(start, width)] = got_ref[:, :width]
    for head in range(KVH):
        columns = slice(width + head * HEAD, width + (head + 1) * HEAD)
        value = sum(got_ref[:, columns].astype(F32) for got_ref in got_refs)
        turned = pltpu.roll(value, HEAD // 2, 1)
        columns = slice(head * HEAD, (head + 1) * HEAD)
        keys_ref[:, columns] = (value * cos_ref[...] + turned * sin_ref[...]).astype(BF16)


def finished(place, cosine, sine, got):
    count, width = got[0].shape
    features = KVH * HEAD
    return pl.pallas_call(
        finish_kernel,
        in_specs=[SMEM] + [VMEM] * (2 + Y),
        out_specs=[VMEM, VMEM],
        out_shape=[
            jax.ShapeDtypeStruct((count, features), BF16),
            jax.ShapeDtypeStruct((count, (width - features) * Y), BF16),
        ],
        compiler_params=PARAMS,
    )(place, cosine, sine, *got)


def swap(value, axis):
    return lax.ppermute(value, axis, [(0, 1), (1, 0)])


def turned_round(value, flip):
    pairs = []
    for y in range(Y):
        for x in range(X):
            for zh in range(ZH):
                source = (y * X + x) * ZH + zh
                pairs.append((source, (x * X + y) * ZH + (zh ^ flip)))
    return lax.ppermute(value, ("y", "x", "zh"), pairs)


def after(value, *others):
    return lax.optimization_barrier((value, *others))[0]


def on_device(tokens, key_codes, key_exponents, key_cotangent):
    y, zl, x, zh, core = [lax.axis_index(name) for name in AXES]
    count = tokens.shape[0]
    features = key_cotangent.shape[1]
    place = jnp.stack([y, zh, core])

    shard = dequantize(key_codes, key_exponents)
    near = turned_round(shard, 0)
    far = turned_round(shard, 1)

    device_index = (((y * ZL + zl) * X + x) * ZH + zh) * CORE + core
    positions = (device_index * count + jnp.arange(count, dtype=jnp.int32)) % SEQ
    cosine, sine = tables(positions)
    packed = packed_for_y(tokens, key_cotangent, cosine, sine)
    got = lax.all_to_all(packed, "y", split_axis=0, concat_axis=0, tiled=True)
    got = after(got, near, far)

    part = partial_products(got, features).reshape(X * CORE, ZL * ZH, ROW, features)
    parts = lax.all_to_all(part, ("x", "core"), split_axis=0, concat_axis=0, tiled=True)

    weights = (near, swap(near, "core"), far, swap(far, "core"))
    applied = apply_weights(place, after(got, part), weights)
    moved = [
        lax.ppermute(applied[k], "y", [(i, (i + k) % Y) for i in range(Y)]) for k in range(1, Y)
    ]

    parts = after(parts, *applied)
    summed = jnp.sum(parts.astype(F32), axis=0).astype(BF16)
    parts = lax.all_to_all(summed, ("zl", "zh"), split_axis=0, concat_axis=0, tiled=True)

    got = [applied[0], *[after(value, summed) for value in moved]]
    keys, input_grad = finished(place, cosine, sine, got)
    parts = after(parts, keys)
    total_tokens = count * Y * ZL * X * ZH * CORE
    weight_grad = jnp.sum(parts.astype(F32), axis=0) * (1.0 / math.sqrt(total_tokens))
    return keys, input_grad, weight_grad


def solution(mesh):
    fine = Mesh(mesh.devices.reshape(Y, ZL, X, ZH, CORE), AXES)
    split = P(AXES, None)
    return jax.shard_map(
        on_device,
        mesh=fine,
        in_specs=(split, P(("x", "zh", "core"), None), P(("x", "zh", "core"), None), split),
        out_specs=(split, split, split),
        check_vma=False,
    )
```

```python
import math

import jax
import jax.numpy as jnp
from jax import lax
from jax.experimental import pallas as pl
from jax.experimental.pallas import tpu as pltpu
from jax.sharding import Mesh
from jax.sharding import PartitionSpec as P

KVH = 4
HEAD = 128
QBLOCK = 256
SEQ = 8192
THETA = 500000.0

Y, ZL, X, ZH, CORE = 4, 8, 4, 2, 2
AXES = ("y", "zl", "x", "zh", "core")
ROW = 8

F32 = jnp.float32
BF16 = jnp.bfloat16
PARAMS = pltpu.CompilerParams(vmem_limit_bytes=20 * 1024 * 1024)
SMEM = pl.BlockSpec(memory_space=pltpu.SMEM)
VMEM = pl.BlockSpec(memory_space=pltpu.VMEM)


def dequantize_kernel(code_ref, exponent_ref, weight_ref):
    scale = jnp.exp2(exponent_ref[...].astype(F32))
    for block in range(code_ref.shape[1] // QBLOCK):
        columns = slice(block * QBLOCK, (block + 1) * QBLOCK)
        value = code_ref[:, columns].astype(F32) * scale[:, block : block + 1]
        weight_ref[:, columns] = value.astype(BF16)


def dequantize(key_codes, key_exponents):
    return pl.pallas_call(
        dequantize_kernel,
        out_shape=jax.ShapeDtypeStruct(key_codes.shape, BF16),
        compiler_params=PARAMS,
    )(key_codes, key_exponents)


def tables(positions):
    inverse = THETA ** (-(jnp.arange(HEAD // 2, dtype=F32) * 2.0 / HEAD))
    angles = positions.astype(F32)[:, None] * inverse[None, :]
    cosine, sine = jnp.cos(angles), jnp.sin(angles)
    return (
        jnp.concatenate([cosine, cosine], axis=1),
        jnp.concatenate([-sine, sine], axis=1),
    )


def pack_kernel(token_ref, cot_ref, cos_ref, sin_ref, packed_ref, pre_ref):
    width = token_ref.shape[1]

    @pl.when(pl.program_id(0) == 0)
    def _():
        for head in range(KVH):
            columns = slice(head * HEAD, (head + 1) * HEAD)
            value = cot_ref[:, columns].astype(F32)
            turned = pltpu.roll(value, HEAD // 2, 1)
            pre_ref[:, columns] = (value * cos_ref[...] - turned * sin_ref[...]).astype(BF16)

    packed_ref[0, :, :width] = token_ref[...]
    packed_ref[0, :, width:] = pre_ref[...]


def packed_for_y(tokens, key_cotangent, cosine, sine):
    count, width = tokens.shape
    features = key_cotangent.shape[1]
    whole = lambda y: (0, 0)
    return pl.pallas_call(
        pack_kernel,
        grid=(Y,),
        in_specs=[
            pl.BlockSpec((count, width // Y), lambda y: (0, y)),
            pl.BlockSpec((count, features), whole),
            pl.BlockSpec((count, HEAD), whole),
            pl.BlockSpec((count, HEAD), whole),
        ],
        out_specs=pl.BlockSpec((1, count, width // Y + features), lambda y: (y, 0, 0)),
        out_shape=jax.ShapeDtypeStruct((Y, count, width // Y + features), BF16),
        scratch_shapes=[pltpu.VMEM((count, features), BF16)],
        compiler_params=PARAMS,
    )(tokens, key_cotangent, cosine, sine)


def partial_kernel(core_ref, token_ref, pre_ref, mine_ref, theirs_ref):
    rows = token_ref.shape[0] * token_ref.shape[1]
    part = lax.dot_general(
        token_ref[...].reshape(rows, token_ref.shape[2]),
        pre_ref[...].reshape(rows, pre_ref.shape[2]),
        (((0,), (0,)), ((), ())),
        preferred_element_type=F32,
    )
    part = part.reshape(-1, CORE, ROW, part.shape[1])
    first = core_ref[0] == 0
    for place in range(mine_ref.shape[0]):
        mine_ref[place] = jnp.where(first, part[place, 0], part[place, 1])
        theirs_ref[place] = jnp.where(first, part[place, 1], part[place, 0]).astype(BF16)


def partial_products(core, got, features):
    count = got.shape[1]
    width = got.shape[2] - features
    steps = 4
    places = ZL * X * ZH
    spec = pl.BlockSpec((places // steps, ROW, features), lambda i: (i, 0, 0))
    return pl.pallas_call(
        partial_kernel,
        grid=(steps,),
        in_specs=[
            SMEM,
            pl.BlockSpec((Y, count, width // steps), lambda i: (0, 0, i)),
            pl.BlockSpec((Y, count, features), lambda i: (0, 0, width // features)),
        ],
        out_specs=[spec, spec],
        out_shape=[
            jax.ShapeDtypeStruct((places, ROW, features), F32),
            jax.ShapeDtypeStruct((places, ROW, features), BF16),
        ],
        compiler_params=PARAMS,
    )(core, got, got)


def apply_kernel(place_ref, got_ref, w00_ref, w01_ref, w10_ref, w11_ref, *out_refs):
    y, zh, core = place_ref[0], place_ref[1], place_ref[2]
    rows, features = w00_ref.shape
    width = ZH * CORE * rows
    held = ((w00_ref, zh, core), (w01_ref, zh, 1 - core), (w10_ref, 1 - zh, core), (w11_ref, 1 - zh, 1 - core))
    for ahead, out_ref in enumerate(out_refs):
        target = lax.rem(y + ahead, Y)
        pre = got_ref[target, :, width:]
        total = jnp.zeros(pre.shape, F32)
        for weight_ref, near, side in held:
            start = pl.multiple_of((near * CORE + side) * rows, rows)
            weight = weight_ref[...]
            total += jnp.dot(
                got_ref[target, :, pl.ds(start, rows)], weight, preferred_element_type=F32
            )
            out_ref[:, pl.ds(start, rows)] = lax.dot_general(
                pre, weight, (((1,), (1,)), ((), ())), preferred_element_type=F32
            ).astype(BF16)
        out_ref[:, width:] = total.astype(BF16)


def apply_weights(place, got, weights):
    count = got.shape[1]
    one = jax.ShapeDtypeStruct((count, got.shape[2]), BF16)
    return pl.pallas_call(
        apply_kernel,
        in_specs=[SMEM] + [VMEM] * 5,
        out_specs=[VMEM] * Y,
        out_shape=[one] * Y,
        compiler_params=PARAMS,
        cost_estimate=pl.CostEstimate(
            flops=2 * 2 * count * Y * got.shape[2] * 512,
            bytes_accessed=6 * 1024 * 1024,
            transcendentals=0,
        ),
    )(place, got, *weights)


def finish_kernel(place_ref, cos_ref, sin_ref, *refs):
    got_refs, keys_ref, grad_ref = refs[:Y], refs[Y], refs[Y + 1]
    width = grad_ref.shape[1] // Y
    for behind, got_ref in enumerate(got_refs):
        source = lax.rem(place_ref[0] + (Y - behind), Y)
        start = pl.multiple_of(source * width, width)
        grad_ref[:, pl.ds(start, width)] = got_ref[:, :width]
    for head in range(KVH):
        columns = slice(width + head * HEAD, width + (head + 1) * HEAD)
        value = sum(got_ref[:, columns].astype(F32) for got_ref in got_refs)
        turned = pltpu.roll(value, HEAD // 2, 1)
        columns = slice(head * HEAD, (head + 1) * HEAD)
        keys_ref[:, columns] = (value * cos_ref[...] + turned * sin_ref[...]).astype(BF16)


def finished(place, cosine, sine, got):
    count, width = got[0].shape
    features = KVH * HEAD
    return pl.pallas_call(
        finish_kernel,
        in_specs=[SMEM] + [VMEM] * (2 + Y),
        out_specs=[VMEM, VMEM],
        out_shape=[
            jax.ShapeDtypeStruct((count, features), BF16),
            jax.ShapeDtypeStruct((count, (width - features) * Y), BF16),
        ],
        compiler_params=PARAMS,
    )(place, cosine, sine, *got)


def swap(value, axis):
    return lax.ppermute(value, axis, [(0, 1), (1, 0)])


def from_column(value, flip):
    offsets = (0, 2, 1, 3)
    pairs = []
    for y in range(Y):
        for x in range(X):
            for zh in range(ZH):
                from_y = (y + offsets[(x - y) % X]) % Y
                source = (from_y * X + y) * ZH + (zh ^ flip)
                pairs.append((source, (y * X + x) * ZH + zh))
    return lax.ppermute(value, ("y", "x", "zh"), pairs)


def after(value, *others):
    return lax.optimization_barrier((value, *others))[0]


def on_device(tokens, key_codes, key_exponents, key_cotangent):
    y, zl, x, zh, core = [lax.axis_index(name) for name in AXES]
    count = tokens.shape[0]
    features = key_cotangent.shape[1]
    place = jnp.stack([y, zh, core])

    shard = dequantize(key_codes, key_exponents)
    near = from_column(shard, 0)
    far = from_column(shard, 1)
    weights = (near, swap(near, "core"), far, swap(far, "core"))

    device_index = (((y * ZL + zl) * X + x) * ZH + zh) * CORE + core
    positions = (device_index * count + jnp.arange(count, dtype=jnp.int32)) % SEQ
    cosine, sine = tables(positions)
    packed = packed_for_y(tokens, key_cotangent, cosine, sine)
    got = lax.all_to_all(packed, "y", split_axis=0, concat_axis=0, tiled=True)
    mine, theirs = partial_products(core[None], got, features)
    other = swap(theirs, "core")
    applied = apply_weights(place, got, weights)
    other = after(other, *applied)
    summed = (mine + other.astype(F32)).astype(BF16)
    parts = lax.all_to_all(summed, ("zl", "x", "zh"), split_axis=0, concat_axis=0, tiled=True)

    moved = [
        lax.ppermute(applied[k], "y", [(i, (i + k) % Y) for i in range(Y)]) for k in range(1, Y)
    ]
    moved = [after(value, summed) for value in moved]
    keys, input_grad = finished(place, cosine, sine, [applied[0], *moved])
    parts = after(parts, keys)
    total_tokens = count * Y * ZL * X * ZH * CORE
    weight_grad = jnp.sum(parts.astype(F32), axis=0) * (1.0 / math.sqrt(total_tokens))
    return keys, input_grad, weight_grad


def solution(mesh):
    fine = Mesh(mesh.devices.reshape(Y, ZL, X, ZH, CORE), AXES)
    split = P(AXES, None)
    return jax.shard_map(
        on_device,
        mesh=fine,
        in_specs=(split, P(("x", "zh", "core"), None), P(("x", "zh", "core"), None), split),
        out_specs=(split, split, split),
        check_vma=False,
    )
```

```python
import math

import jax
import jax.numpy as jnp
from jax import lax
from jax.experimental import pallas as pl
from jax.experimental.pallas import tpu as pltpu
from jax.sharding import Mesh
from jax.sharding import PartitionSpec as P

KVH = 4
HEAD = 128
QBLOCK = 256
SEQ = 8192
THETA = 500000.0

Y, ZL, X, ZH, CORE = 4, 8, 4, 2, 2
AXES = ("y", "zl", "x", "zh", "core")
ROW = 8

F32 = jnp.float32
BF16 = jnp.bfloat16
PARAMS = pltpu.CompilerParams(vmem_limit_bytes=20 * 1024 * 1024)
SMEM = pl.BlockSpec(memory_space=pltpu.SMEM)
VMEM = pl.BlockSpec(memory_space=pltpu.VMEM)


def dequantize_kernel(code_ref, exponent_ref, weight_ref):
    scale = jnp.exp2(exponent_ref[...].astype(F32))
    for block in range(code_ref.shape[1] // QBLOCK):
        columns = slice(block * QBLOCK, (block + 1) * QBLOCK)
        value = code_ref[:, columns].astype(F32) * scale[:, block : block + 1]
        weight_ref[:, columns] = value.astype(BF16)


def dequantize(key_codes, key_exponents):
    return pl.pallas_call(
        dequantize_kernel,
        out_shape=jax.ShapeDtypeStruct(key_codes.shape, BF16),
        compiler_params=PARAMS,
    )(key_codes, key_exponents)


def tables(positions):
    inverse = THETA ** (-(jnp.arange(HEAD // 2, dtype=F32) * 2.0 / HEAD))
    angles = positions.astype(F32)[:, None] * inverse[None, :]
    cosine, sine = jnp.cos(angles), jnp.sin(angles)
    return (
        jnp.concatenate([cosine, cosine], axis=1),
        jnp.concatenate([-sine, sine], axis=1),
    )


def pack_kernel(token_ref, cot_ref, cos_ref, sin_ref, packed_ref, pre_ref):
    width = token_ref.shape[1]

    @pl.when(pl.program_id(0) == 0)
    def _():
        for head in range(KVH):
            columns = slice(head * HEAD, (head + 1) * HEAD)
            value = cot_ref[:, columns].astype(F32)
            turned = pltpu.roll(value, HEAD // 2, 1)
            pre_ref[:, columns] = (value * cos_ref[...] - turned * sin_ref[...]).astype(BF16)

    packed_ref[0, :, :width] = token_ref[...]
    packed_ref[0, :, width:] = pre_ref[...]


def packed_for_x(tokens, key_cotangent, cosine, sine):
    count, width = tokens.shape
    features = key_cotangent.shape[1]
    whole = lambda x: (0, 0)
    return pl.pallas_call(
        pack_kernel,
        grid=(X,),
        in_specs=[
            pl.BlockSpec((count, width // X), lambda x: (0, x)),
            pl.BlockSpec((count, features), whole),
            pl.BlockSpec((count, HEAD), whole),
            pl.BlockSpec((count, HEAD), whole),
        ],
        out_specs=pl.BlockSpec((1, count, width // X + features), lambda x: (x, 0, 0)),
        out_shape=jax.ShapeDtypeStruct((X, count, width // X + features), BF16),
        scratch_shapes=[pltpu.VMEM((count, features), BF16)],
        compiler_params=PARAMS,
    )(tokens, key_cotangent, cosine, sine)


def partial_kernel(core_ref, token_ref, pre_ref, mine_ref, theirs_ref):
    rows = token_ref.shape[0] * token_ref.shape[1]
    part = lax.dot_general(
        token_ref[...].reshape(rows, token_ref.shape[2]),
        pre_ref[...].reshape(rows, pre_ref.shape[2]),
        (((0,), (0,)), ((), ())),
        preferred_element_type=F32,
    )
    part = part.reshape(-1, CORE, ROW, part.shape[1])
    first = core_ref[0] == 0
    for zl in range(mine_ref.shape[1]):
        for owner in range(X):
            for zh in range(ZH):
                place = (zl * X + owner) * ZH + zh
                one, two = part[place, 0], part[place, 1]
                mine_ref[owner, zl, zh] = jnp.where(first, one, two)
                theirs_ref[owner, zl, zh] = jnp.where(first, two, one).astype(BF16)


def partial_products(core, got, features):
    count = got.shape[1]
    width = got.shape[2] - features
    steps = 4
    shape = (X, ZL, ZH, ROW, features)
    spec = pl.BlockSpec((X, ZL // steps, ZH, ROW, features), lambda i: (0, i, 0, 0, 0))
    return pl.pallas_call(
        partial_kernel,
        grid=(steps,),
        in_specs=[
            SMEM,
            pl.BlockSpec((X, count, width // steps), lambda i: (0, 0, i)),
            pl.BlockSpec((X, count, features), lambda i: (0, 0, width // features)),
        ],
        out_specs=[spec, spec],
        out_shape=[jax.ShapeDtypeStruct(shape, F32), jax.ShapeDtypeStruct(shape, BF16)],
        compiler_params=PARAMS,
    )(core, got, got)


def apply_kernel(place_ref, got_ref, w00_ref, w01_ref, w10_ref, w11_ref, *out_refs):
    x, zh, core = place_ref[0], place_ref[1], place_ref[2]
    rows, features = w00_ref.shape
    width = ZH * CORE * rows
    held = ((w00_ref, zh, core), (w01_ref, zh, 1 - core), (w10_ref, 1 - zh, core), (w11_ref, 1 - zh, 1 - core))
    for ahead, out_ref in enumerate(out_refs):
        target = lax.rem(x + ahead, X)
        pre = got_ref[target, :, width:]
        total = jnp.zeros(pre.shape, F32)
        for weight_ref, near, side in held:
            start = pl.multiple_of((near * CORE + side) * rows, rows)
            weight = weight_ref[...]
            total += jnp.dot(
                got_ref[target, :, pl.ds(start, rows)], weight, preferred_element_type=F32
            )
            out_ref[:, pl.ds(start, rows)] = lax.dot_general(
                pre, weight, (((1,), (1,)), ((), ())), preferred_element_type=F32
            ).astype(BF16)
        out_ref[:, width:] = total.astype(BF16)


def apply_weights(place, got, weights):
    count = got.shape[1]
    one = jax.ShapeDtypeStruct((count, got.shape[2]), BF16)
    return pl.pallas_call(
        apply_kernel,
        in_specs=[SMEM] + [VMEM] * 5,
        out_specs=[VMEM] * X,
        out_shape=[one] * X,
        compiler_params=PARAMS,
        cost_estimate=pl.CostEstimate(
            flops=2 * 2 * count * X * got.shape[2] * 512,
            bytes_accessed=6 * 1024 * 1024,
            transcendentals=0,
        ),
    )(place, got, *weights)


def finish_kernel(place_ref, cos_ref, sin_ref, *refs):
    got_refs, keys_ref, grad_ref = refs[:X], refs[X], refs[X + 1]
    width = grad_ref.shape[1] // X
    for behind, got_ref in enumerate(got_refs):
        source = lax.rem(place_ref[0] + (X - behind), X)
        start = pl.multiple_of(source * width, width)
        grad_ref[:, pl.ds(start, width)] = got_ref[:, :width]
    for head in range(KVH):
        columns = slice(width + head * HEAD, width + (head + 1) * HEAD)
        value = sum(got_ref[:, columns].astype(F32) for got_ref in got_refs)
        turned = pltpu.roll(value, HEAD // 2, 1)
        columns = slice(head * HEAD, (head + 1) * HEAD)
        keys_ref[:, columns] = (value * cos_ref[...] + turned * sin_ref[...]).astype(BF16)


def finished(place, cosine, sine, got):
    count, width = got[0].shape
    features = KVH * HEAD
    return pl.pallas_call(
        finish_kernel,
        in_specs=[SMEM] + [VMEM] * (2 + X),
        out_specs=[VMEM, VMEM],
        out_shape=[
            jax.ShapeDtypeStruct((count, features), BF16),
            jax.ShapeDtypeStruct((count, (width - features) * X), BF16),
        ],
        compiler_params=PARAMS,
        cost_estimate=pl.CostEstimate(flops=100000000000, bytes_accessed=2 * 1024 * 1024, transcendentals=0),
    )(place, cosine, sine, *got)


def swap(value, axis):
    return lax.ppermute(value, axis, [(0, 1), (1, 0)])


def after(value, *others):
    return lax.optimization_barrier((value, *others))[0]


def on_device(tokens, key_codes, key_exponents, key_cotangent):
    y, zl, x, zh, core = [lax.axis_index(name) for name in AXES]
    count = tokens.shape[0]
    features = key_cotangent.shape[1]
    place = jnp.stack([x, zh, core])

    shard = dequantize(key_codes, key_exponents)
    far = swap(shard, "zh")
    weights = (shard, swap(shard, "core"), far, swap(far, "core"))

    device_index = (((y * ZL + zl) * X + x) * ZH + zh) * CORE + core
    positions = (device_index * count + jnp.arange(count, dtype=jnp.int32)) % SEQ
    cosine, sine = tables(positions)
    packed = packed_for_x(after(tokens, shard), key_cotangent, cosine, sine)
    got = lax.all_to_all(packed, "x", split_axis=0, concat_axis=0, tiled=True)
    got = after(got, far, weights[1])
    mine, theirs = partial_products(core[None], got, features)
    other = swap(theirs, "core")
    summed = (mine + other.astype(F32)).astype(BF16).reshape(X, ZL * ZH, ROW, features)
    parts = lax.all_to_all(summed, "y", split_axis=0, concat_axis=0, tiled=True)
    got = after(got, summed)
    applied = apply_weights(place, got, weights)
    moved = [
        lax.ppermute(applied[k], "x", [(i, (i + k) % X) for i in range(X)]) for k in range(1, X)
    ]
    parts = after(parts, *applied)
    summed = jnp.sum(parts.astype(F32), axis=0).astype(BF16)
    parts = lax.all_to_all(summed, ("zl", "zh"), split_axis=0, concat_axis=0, tiled=True)
    keys, input_grad = finished(place, cosine, sine, [applied[0], *moved])
    parts = after(parts, keys)
    total_tokens = count * Y * ZL * X * ZH * CORE
    weight_grad = jnp.sum(parts.astype(F32), axis=0) * (1.0 / math.sqrt(total_tokens))
    pairs = [(i * X + j, j * X + i) for i in range(Y) for j in range(X)]
    weight_grad = lax.ppermute(weight_grad, ("y", "x"), pairs)
    return keys, input_grad, weight_grad


def solution(mesh):
    fine = Mesh(mesh.devices.reshape(Y, ZL, X, ZH, CORE), AXES)
    split = P(AXES, None)
    return jax.shard_map(
        on_device,
        mesh=fine,
        in_specs=(split, P(("x", "zh", "core"), None), P(("x", "zh", "core"), None), split),
        out_specs=(split, split, split),
        check_vma=False,
    )
```

```python
import functools
import math

import jax
import jax.numpy as jnp
from jax import lax
from jax.experimental import pallas as pl
from jax.experimental.pallas import tpu as pltpu
from jax.sharding import Mesh
from jax.sharding import PartitionSpec as P

KVH = 4
HEAD = 128
QBLOCK = 256
SEQ = 8192
THETA = 500000.0

Y, ZL, X, ZH, CORE = 4, 8, 4, 2, 2
AXES = ("y", "zl", "x", "zh", "core")
ROW = 8

F32 = jnp.float32
BF16 = jnp.bfloat16
PARAMS = pltpu.CompilerParams(vmem_limit_bytes=20 * 1024 * 1024)


def dequantize_kernel(code_ref, exponent_ref, weight_ref):
    scale = jnp.exp2(exponent_ref[...].astype(F32))
    for block in range(code_ref.shape[1] // QBLOCK):
        columns = slice(block * QBLOCK, (block + 1) * QBLOCK)
        value = code_ref[:, columns].astype(F32) * scale[:, block : block + 1]
        weight_ref[:, columns] = value.astype(BF16)


def dequantize(key_codes, key_exponents):
    return pl.pallas_call(
        dequantize_kernel,
        out_shape=jax.ShapeDtypeStruct(key_codes.shape, BF16),
        compiler_params=PARAMS,
    )(key_codes, key_exponents)


def tables(positions):
    inverse = THETA ** (-(jnp.arange(HEAD // 2, dtype=F32) * 2.0 / HEAD))
    angles = positions.astype(F32)[:, None] * inverse[None, :]
    cosine, sine = jnp.cos(angles), jnp.sin(angles)
    return (
        jnp.concatenate([cosine, cosine], axis=1),
        jnp.concatenate([-sine, sine], axis=1),
    )


def partial_kernel(core_ref, token_ref, cot_ref, cos_ref, sin_ref, mine_ref, theirs_ref, pre_ref, part_ref):
    @pl.when(pl.program_id(0) == 0)
    def _():
        for head in range(KVH):
            columns = slice(head * HEAD, (head + 1) * HEAD)
            value = cot_ref[:, columns].astype(F32)
            turned = pltpu.roll(value, HEAD // 2, 1)
            pre_ref[:, columns] = (value * cos_ref[...] - turned * sin_ref[...]).astype(BF16)

    part = lax.dot_general(
        token_ref[...], pre_ref[...], (((0,), (0,)), ((), ())), preferred_element_type=F32
    )
    part_ref[...] = part.reshape(part_ref.shape)
    core = core_ref[0]
    for x in range(X):
        for zl in range(ZL):
            for zh in range(ZH):
                place = (zl * X + x) * ZH + zh
                mine_ref[0, x, zl, zh] = part_ref[place, core].astype(BF16)
                theirs_ref[0, x, zl, zh] = part_ref[place, 1 - core].astype(BF16)


def partial_products(core, tokens, key_cotangent, cosine, sine):
    count, width = tokens.shape
    features = key_cotangent.shape[1]
    step = width // Y
    half = jax.ShapeDtypeStruct((Y, X, ZL, ZH, ROW, features), BF16)
    half_spec = pl.BlockSpec((1, X, ZL, ZH, ROW, features), lambda y: (y, 0, 0, 0, 0, 0))
    whole = lambda y: (0, 0)
    return pl.pallas_call(
        partial_kernel,
        grid=(Y,),
        in_specs=[
            pl.BlockSpec(memory_space=pltpu.SMEM),
            pl.BlockSpec((count, step), lambda y: (0, y)),
            pl.BlockSpec((count, features), whole),
            pl.BlockSpec((count, HEAD), whole),
            pl.BlockSpec((count, HEAD), whole),
        ],
        out_specs=[half_spec, half_spec, pl.BlockSpec((count, features), whole)],
        out_shape=[half, half, jax.ShapeDtypeStruct((count, features), BF16)],
        scratch_shapes=[pltpu.VMEM((ZL * X * ZH, CORE, ROW, features), F32)],
        compiler_params=PARAMS,
    )(core, tokens, key_cotangent, cosine, sine)


def join_kernel(*refs):
    rows = refs[0].shape[0]
    for block, ref in enumerate(refs[:-1]):
        refs[-1][block * rows : (block + 1) * rows, :] = ref[...]


def joined(blocks):
    rows, features = blocks[0].shape
    return pl.pallas_call(
        join_kernel,
        out_shape=jax.ShapeDtypeStruct((len(blocks) * rows, features), BF16),
        compiler_params=PARAMS,
        cost_estimate=pl.CostEstimate(flops=100000000000, bytes_accessed=4 * 1024 * 1024, transcendentals=0),
    )(*blocks)


def first_column(place_ref, block, side, rows):
    x, zh = place_ref[0], place_ref[1]
    near = zh if block < X else 1 - zh
    source = lax.rem(x + (X - block % X), X)
    return pl.multiple_of(((source * ZH + near) * CORE + side) * rows, rows)


def apply_first_kernel(place_ref, token_ref, pre_ref, weight_ref, total_ref, grad_ref):
    rows = weight_ref.shape[0] // (ZH * X)
    pre = pre_ref[...]
    total = jnp.zeros(pre.shape, F32)
    for block in range(ZH * X):
        start = first_column(place_ref, block, place_ref[2], rows)
        weight = weight_ref[block * rows : (block + 1) * rows, :]
        total += jnp.dot(token_ref[:, pl.ds(start, rows)], weight, preferred_element_type=F32)
        grad_ref[block] = lax.dot_general(
            pre, weight, (((1,), (1,)), ((), ())), preferred_element_type=F32
        ).astype(BF16)
    total_ref[...] = total


def apply_second_kernel(place_ref, token_ref, pre_ref, cos_ref, sin_ref, weight_ref, total_ref, half_ref, keys_ref, grad_ref):
    rows = weight_ref.shape[0] // (ZH * X)
    pre = pre_ref[...]
    total = total_ref[...]
    for block in range(ZH * X):
        start = first_column(place_ref, block, place_ref[2], rows)
        grad_ref[:, pl.ds(start, rows)] = half_ref[block]
        start = first_column(place_ref, block, 1 - place_ref[2], rows)
        weight = weight_ref[block * rows : (block + 1) * rows, :]
        total += jnp.dot(token_ref[:, pl.ds(start, rows)], weight, preferred_element_type=F32)
        grad_ref[:, pl.ds(start, rows)] = lax.dot_general(
            pre, weight, (((1,), (1,)), ((), ())), preferred_element_type=F32
        ).astype(BF16)
    for head in range(KVH):
        columns = slice(head * HEAD, (head + 1) * HEAD)
        value = total[:, columns]
        turned = pltpu.roll(value, HEAD // 2, 1)
        keys_ref[:, columns] = (value * cos_ref[...] + turned * sin_ref[...]).astype(BF16)


def product_cost(tokens, features):
    return pl.CostEstimate(
        flops=2 * tokens.shape[0] * tokens.shape[1] * features,
        bytes_accessed=4 * 1024 * 1024,
        transcendentals=0,
    )


def apply_first(place, tokens, pre_grad, weights):
    vmem = pl.BlockSpec(memory_space=pltpu.VMEM)
    count, features = pre_grad.shape
    blocks = ZH * X
    return pl.pallas_call(
        apply_first_kernel,
        in_specs=[pl.BlockSpec(memory_space=pltpu.SMEM)] + [vmem] * 3,
        out_specs=[vmem, vmem],
        out_shape=[
            jax.ShapeDtypeStruct((count, features), F32),
            jax.ShapeDtypeStruct((blocks, count, weights.shape[0] // blocks), BF16),
        ],
        compiler_params=PARAMS,
        cost_estimate=pl.CostEstimate(flops=100000000000, bytes_accessed=4 * 1024 * 1024, transcendentals=0),
    )(place, tokens, pre_grad, weights)


def apply_second(place, tokens, pre_grad, cosine, sine, weights, total, half):
    vmem = pl.BlockSpec(memory_space=pltpu.VMEM)
    return pl.pallas_call(
        apply_second_kernel,
        in_specs=[pl.BlockSpec(memory_space=pltpu.SMEM)] + [vmem] * 7,
        out_specs=[vmem, vmem],
        out_shape=[
            jax.ShapeDtypeStruct(pre_grad.shape, BF16),
            jax.ShapeDtypeStruct(tokens.shape, BF16),
        ],
        compiler_params=PARAMS,
        cost_estimate=product_cost(tokens, pre_grad.shape[1]),
    )(place, tokens, pre_grad, cosine, sine, weights, total, half)


def after(value, *others):
    return lax.optimization_barrier((value, *others))[0]


def from_x(shard):
    moved = [lax.ppermute(shard, "x", [(i, (i + k) % X) for i in range(X)]) for k in range(1, X)]
    return [shard, *moved]


def sum_kernel(factor, *refs):
    total = refs[0][0].astype(F32)
    for ref in refs[:-1]:
        for place in range(ref.shape[0]):
            if ref is not refs[0] or place:
                total += ref[place].astype(F32)
    refs[-1][...] = (total * factor).astype(refs[-1].dtype)


def summed_first(*parts, dtype=BF16, factor=1.0, steps=1):
    shape = parts[0].shape[1:]
    block = (shape[0] // steps, *shape[1:])
    rest = (0,) * (len(shape) - 1)
    return pl.pallas_call(
        functools.partial(sum_kernel, factor),
        grid=(steps,),
        in_specs=[pl.BlockSpec((part.shape[0], *block), lambda i: (0, i, *rest)) for part in parts],
        out_specs=pl.BlockSpec(block, lambda i: (i, *rest)),
        out_shape=jax.ShapeDtypeStruct(shape, dtype),
        compiler_params=PARAMS,
    )(*parts)


def swap(value, axis):
    return lax.ppermute(value, axis, [(0, 1), (1, 0)])


def on_device(tokens, key_codes, key_exponents, key_cotangent):
    y, zl, x, zh, core = [lax.axis_index(name) for name in AXES]
    count = tokens.shape[0]
    features = key_cotangent.shape[1]

    shard = dequantize(key_codes, key_exponents)
    device_index = (((y * ZL + zl) * X + x) * ZH + zh) * CORE + core
    positions = (device_index * count + jnp.arange(count, dtype=jnp.int32)) % SEQ
    cosine, sine = tables(positions)
    mine, theirs, pre_grad = partial_products(core[None], after(tokens, shard), key_cotangent, cosine, sine)

    flat = (1, Y * X * ZL * ZH, ROW, features)
    summed = summed_first(mine.reshape(flat), swap(theirs, "core").reshape(flat), steps=8)
    summed = summed.reshape(Y, X * ZL * ZH, ROW, features)
    got = lax.all_to_all(summed, "y", split_axis=0, concat_axis=0, tiled=True)

    shard = after(shard, theirs)
    far_shard = after(swap(shard, "zh"), summed)
    near = from_x(shard)
    far = from_x(far_shard)

    summed = summed_first(got, steps=4).reshape(X, ZL * ZH, ROW, features)
    got = lax.all_to_all(summed, "x", split_axis=0, concat_axis=0, tiled=True)

    held = joined(near + far)
    swapped = swap(held, "core")
    summed = after(summed_first(got, steps=2), held)
    got = lax.all_to_all(summed, ("zl", "zh"), split_axis=0, concat_axis=0, tiled=True)

    place = jnp.stack([x, zh, core])
    total, half = apply_first(place, tokens, pre_grad, held)
    keys, input_grad = apply_second(
        place, tokens, pre_grad, cosine, sine, swapped, total, half
    )
    got = after(got, keys)
    total_tokens = count * Y * ZL * X * ZH * CORE
    weight_grad = summed_first(got, dtype=F32, factor=1.0 / math.sqrt(total_tokens))
    return keys, input_grad, weight_grad


def solution(mesh):
    fine = Mesh(mesh.devices.reshape(Y, ZL, X, ZH, CORE), AXES)
    split = P(AXES, None)
    return jax.shard_map(
        on_device,
        mesh=fine,
        in_specs=(split, P(("x", "zh", "core"), None), P(("x", "zh", "core"), None), split),
        out_specs=(split, split, split),
        check_vma=False,
    )
```

```python
import functools
import math

import jax
import jax.numpy as jnp
from jax import lax
from jax.experimental import pallas as pl
from jax.experimental.pallas import tpu as pltpu
from jax.sharding import Mesh
from jax.sharding import PartitionSpec as P

KVH = 4
HEAD = 128
QBLOCK = 256
SEQ = 8192
THETA = 500000.0

Y, ZL, X, ZH, CORE = 4, 8, 4, 2, 2
AXES = ("y", "zl", "x", "zh", "core")
ROW = 8

F32 = jnp.float32
BF16 = jnp.bfloat16
PARAMS = pltpu.CompilerParams(vmem_limit_bytes=20 * 1024 * 1024)


def dequantize_kernel(code_ref, exponent_ref, weight_ref):
    scale = jnp.exp2(exponent_ref[...].astype(F32))
    for block in range(code_ref.shape[1] // QBLOCK):
        columns = slice(block * QBLOCK, (block + 1) * QBLOCK)
        value = code_ref[:, columns].astype(F32) * scale[:, block : block + 1]
        weight_ref[:, columns] = value.astype(BF16)


def dequantize(key_codes, key_exponents):
    return pl.pallas_call(
        dequantize_kernel,
        out_shape=jax.ShapeDtypeStruct(key_codes.shape, BF16),
        compiler_params=PARAMS,
    )(key_codes, key_exponents)


def tables(positions):
    inverse = THETA ** (-(jnp.arange(HEAD // 2, dtype=F32) * 2.0 / HEAD))
    angles = positions.astype(F32)[:, None] * inverse[None, :]
    cosine, sine = jnp.cos(angles), jnp.sin(angles)
    return (
        jnp.concatenate([cosine, cosine], axis=1),
        jnp.concatenate([-sine, sine], axis=1),
    )


def partial_kernel(core_ref, token_ref, cot_ref, cos_ref, sin_ref, mine_ref, theirs_ref, pre_ref, part_ref):
    @pl.when(pl.program_id(0) == 0)
    def _():
        for head in range(KVH):
            columns = slice(head * HEAD, (head + 1) * HEAD)
            value = cot_ref[:, columns].astype(F32)
            turned = pltpu.roll(value, HEAD // 2, 1)
            pre_ref[:, columns] = (value * cos_ref[...] - turned * sin_ref[...]).astype(BF16)

    part = lax.dot_general(
        token_ref[...], pre_ref[...], (((0,), (0,)), ((), ())), preferred_element_type=F32
    )
    part_ref[...] = part.reshape(part_ref.shape)
    core = core_ref[0]
    for x in range(X):
        for zl in range(ZL):
            for zh in range(ZH):
                place = (zl * X + x) * ZH + zh
                mine_ref[0, x, zl, zh] = part_ref[place, core].astype(BF16)
                theirs_ref[0, x, zl, zh] = part_ref[place, 1 - core].astype(BF16)


def partial_products(core, tokens, key_cotangent, cosine, sine):
    count, width = tokens.shape
    features = key_cotangent.shape[1]
    step = width // Y
    half = jax.ShapeDtypeStruct((Y, X, ZL, ZH, ROW, features), BF16)
    half_spec = pl.BlockSpec((1, X, ZL, ZH, ROW, features), lambda y: (y, 0, 0, 0, 0, 0))
    whole = lambda y: (0, 0)
    return pl.pallas_call(
        partial_kernel,
        grid=(Y,),
        in_specs=[
            pl.BlockSpec(memory_space=pltpu.SMEM),
            pl.BlockSpec((count, step), lambda y: (0, y)),
            pl.BlockSpec((count, features), whole),
            pl.BlockSpec((count, HEAD), whole),
            pl.BlockSpec((count, HEAD), whole),
        ],
        out_specs=[half_spec, half_spec, pl.BlockSpec((count, features), whole)],
        out_shape=[half, half, jax.ShapeDtypeStruct((count, features), BF16)],
        scratch_shapes=[pltpu.VMEM((ZL * X * ZH, CORE, ROW, features), F32)],
        compiler_params=PARAMS,
    )(core, tokens, key_cotangent, cosine, sine)


def join_kernel(*refs):
    rows = refs[0].shape[0]
    for block, ref in enumerate(refs[:-1]):
        refs[-1][block * rows : (block + 1) * rows, :] = ref[...]


def joined(blocks):
    rows, features = blocks[0].shape
    return pl.pallas_call(
        join_kernel,
        out_shape=jax.ShapeDtypeStruct((len(blocks) * rows, features), BF16),
        compiler_params=PARAMS,
        cost_estimate=pl.CostEstimate(flops=100000000000, bytes_accessed=4 * 1024 * 1024, transcendentals=0),
    )(*blocks)


def relay_kernel(block_ref, out_ref):
    out_ref[...] = block_ref[...]


def relayed(block):
    return pl.pallas_call(
        relay_kernel,
        out_shape=jax.ShapeDtypeStruct(block.shape, block.dtype),
        compiler_params=PARAMS,
        cost_estimate=pl.CostEstimate(
            flops=100000000000, bytes_accessed=512 * 1024, transcendentals=0
        ),
    )(block)


def first_column(place_ref, block, side, rows):
    x, zh = place_ref[0], place_ref[1]
    near = zh if block < X else 1 - zh
    source = lax.rem(x + (X - block % X), X)
    return pl.multiple_of(((source * ZH + near) * CORE + side) * rows, rows)


def apply_first_kernel(place_ref, token_ref, pre_ref, weight_ref, total_ref, grad_ref):
    rows = weight_ref.shape[0] // (ZH * X)
    pre = pre_ref[...]
    total = jnp.zeros(pre.shape, F32)
    for block in range(ZH * X):
        start = first_column(place_ref, block, place_ref[2], rows)
        weight = weight_ref[block * rows : (block + 1) * rows, :]
        total += jnp.dot(token_ref[:, pl.ds(start, rows)], weight, preferred_element_type=F32)
        grad_ref[block] = lax.dot_general(
            pre, weight, (((1,), (1,)), ((), ())), preferred_element_type=F32
        ).astype(BF16)
    total_ref[...] = total


def apply_second_kernel(place_ref, token_ref, pre_ref, cos_ref, sin_ref, weight_ref, total_ref, half_ref, keys_ref, grad_ref):
    rows = weight_ref.shape[0] // (ZH * X)
    pre = pre_ref[...]
    total = total_ref[...]
    for block in range(ZH * X):
        start = first_column(place_ref, block, place_ref[2], rows)
        grad_ref[:, pl.ds(start, rows)] = half_ref[block]
        start = first_column(place_ref, block, 1 - place_ref[2], rows)
        weight = weight_ref[block * rows : (block + 1) * rows, :]
        total += jnp.dot(token_ref[:, pl.ds(start, rows)], weight, preferred_element_type=F32)
        grad_ref[:, pl.ds(start, rows)] = lax.dot_general(
            pre, weight, (((1,), (1,)), ((), ())), preferred_element_type=F32
        ).astype(BF16)
    for head in range(KVH):
        columns = slice(head * HEAD, (head + 1) * HEAD)
        value = total[:, columns]
        turned = pltpu.roll(value, HEAD // 2, 1)
        keys_ref[:, columns] = (value * cos_ref[...] + turned * sin_ref[...]).astype(BF16)


def product_cost(tokens, features):
    return pl.CostEstimate(
        flops=2 * tokens.shape[0] * tokens.shape[1] * features,
        bytes_accessed=4 * 1024 * 1024,
        transcendentals=0,
    )


def apply_first(place, tokens, pre_grad, weights):
    vmem = pl.BlockSpec(memory_space=pltpu.VMEM)
    count, features = pre_grad.shape
    blocks = ZH * X
    return pl.pallas_call(
        apply_first_kernel,
        in_specs=[pl.BlockSpec(memory_space=pltpu.SMEM)] + [vmem] * 3,
        out_specs=[vmem, vmem],
        out_shape=[
            jax.ShapeDtypeStruct((count, features), F32),
            jax.ShapeDtypeStruct((blocks, count, weights.shape[0] // blocks), BF16),
        ],
        compiler_params=PARAMS,
        cost_estimate=pl.CostEstimate(flops=100000000000, bytes_accessed=4 * 1024 * 1024, transcendentals=0),
    )(place, tokens, pre_grad, weights)


def apply_second(place, tokens, pre_grad, cosine, sine, weights, total, half):
    vmem = pl.BlockSpec(memory_space=pltpu.VMEM)
    return pl.pallas_call(
        apply_second_kernel,
        in_specs=[pl.BlockSpec(memory_space=pltpu.SMEM)] + [vmem] * 7,
        out_specs=[vmem, vmem],
        out_shape=[
            jax.ShapeDtypeStruct(pre_grad.shape, BF16),
            jax.ShapeDtypeStruct(tokens.shape, BF16),
        ],
        compiler_params=PARAMS,
        cost_estimate=product_cost(tokens, pre_grad.shape[1]),
    )(place, tokens, pre_grad, cosine, sine, weights, total, half)


def after(value, *others):
    return lax.optimization_barrier((value, *others))[0]


def from_x(shard):
    moved = [lax.ppermute(shard, "x", [(i, (i + k) % X) for i in range(X)]) for k in range(1, X)]
    return [shard, *moved]


def sum_kernel(factor, *refs):
    total = refs[0][0].astype(F32)
    for ref in refs[:-1]:
        for place in range(ref.shape[0]):
            if ref is not refs[0] or place:
                total += ref[place].astype(F32)
    refs[-1][...] = (total * factor).astype(refs[-1].dtype)


def summed_first(*parts, dtype=BF16, factor=1.0, steps=1):
    shape = parts[0].shape[1:]
    block = (shape[0] // steps, *shape[1:])
    rest = (0,) * (len(shape) - 1)
    return pl.pallas_call(
        functools.partial(sum_kernel, factor),
        grid=(steps,),
        in_specs=[pl.BlockSpec((part.shape[0], *block), lambda i: (0, i, *rest)) for part in parts],
        out_specs=pl.BlockSpec(block, lambda i: (i, *rest)),
        out_shape=jax.ShapeDtypeStruct(shape, dtype),
        compiler_params=PARAMS,
    )(*parts)


def swap(value, axis):
    return lax.ppermute(value, axis, [(0, 1), (1, 0)])


def on_device(tokens, key_codes, key_exponents, key_cotangent):
    y, zl, x, zh, core = [lax.axis_index(name) for name in AXES]
    count = tokens.shape[0]
    features = key_cotangent.shape[1]

    shard = dequantize(key_codes, key_exponents)
    device_index = (((y * ZL + zl) * X + x) * ZH + zh) * CORE + core
    positions = (device_index * count + jnp.arange(count, dtype=jnp.int32)) % SEQ
    cosine, sine = tables(positions)
    mine, theirs, pre_grad = partial_products(core[None], after(tokens, shard), key_cotangent, cosine, sine)

    flat = (1, Y * X * ZL * ZH, ROW, features)
    summed = summed_first(mine.reshape(flat), swap(theirs, "core").reshape(flat), steps=8)
    summed = summed.reshape(Y, X * ZL * ZH, ROW, features)
    got = lax.all_to_all(summed, "y", split_axis=0, concat_axis=0, tiled=True)

    shard = after(shard, theirs)
    far_shard = relayed(after(swap(shard, "zh"), summed))
    near = from_x(after(shard, summed))
    far = from_x(far_shard)

    summed = summed_first(got, steps=4).reshape(X, ZL * ZH, ROW, features)
    got = lax.all_to_all(summed, "x", split_axis=0, concat_axis=0, tiled=True)

    held = joined(near + far)
    swapped = swap(held, "core")
    summed = after(summed_first(got, steps=2), held)
    got = lax.all_to_all(summed, ("zl", "zh"), split_axis=0, concat_axis=0, tiled=True)

    place = jnp.stack([x, zh, core])
    total, half = apply_first(place, tokens, pre_grad, held)
    keys, input_grad = apply_second(
        place, tokens, pre_grad, cosine, sine, swapped, total, half
    )
    got = after(got, keys)
    total_tokens = count * Y * ZL * X * ZH * CORE
    weight_grad = summed_first(got, dtype=F32, factor=1.0 / math.sqrt(total_tokens))
    return keys, input_grad, weight_grad


def solution(mesh):
    fine = Mesh(mesh.devices.reshape(Y, ZL, X, ZH, CORE), AXES)
    split = P(AXES, None)
    return jax.shard_map(
        on_device,
        mesh=fine,
        in_specs=(split, P(("x", "zh", "core"), None), P(("x", "zh", "core"), None), split),
        out_specs=(split, split, split),
        check_vma=False,
    )
```

```python
import functools
import math

import jax
import jax.numpy as jnp
from jax import lax
from jax.experimental import pallas as pl
from jax.experimental.pallas import tpu as pltpu
from jax.sharding import Mesh
from jax.sharding import PartitionSpec as P

KVH = 4
HEAD = 128
QBLOCK = 256
SEQ = 8192
THETA = 500000.0

Y, ZL, X, ZH, CORE = 4, 8, 4, 2, 2
AXES = ("y", "zl", "x", "zh", "core")
ROW = 8

F32 = jnp.float32
BF16 = jnp.bfloat16
PARAMS = pltpu.CompilerParams(vmem_limit_bytes=20 * 1024 * 1024)


def dequantize_kernel(code_ref, exponent_ref, weight_ref):
    rows = code_ref.shape[0]
    scale = jnp.exp2(exponent_ref[...].astype(F32))
    same = lax.broadcasted_iota(jnp.int32, (rows, rows), 0) == lax.broadcasted_iota(
        jnp.int32, (rows, rows), 1
    )
    for block in range(code_ref.shape[1] // QBLOCK):
        columns = slice(block * QBLOCK, (block + 1) * QBLOCK)
        down = jnp.sum(jnp.where(same, scale[block : block + 1, :], 0.0), axis=1, keepdims=True)
        weight_ref[:, columns] = (code_ref[:, columns].astype(F32) * down).astype(BF16)


def dequantize(key_codes, key_exponents):
    return pl.pallas_call(
        dequantize_kernel,
        out_shape=jax.ShapeDtypeStruct(key_codes.shape, BF16),
        compiler_params=PARAMS,
    )(key_codes, key_exponents.T)


def tables(positions):
    inverse = THETA ** (-(jnp.arange(HEAD // 2, dtype=F32) * 2.0 / HEAD))
    angles = positions.astype(F32)[:, None] * inverse[None, :]
    cosine, sine = jnp.cos(angles), jnp.sin(angles)
    return (
        jnp.concatenate([cosine, cosine], axis=1),
        jnp.concatenate([-sine, sine], axis=1),
    )


def partial_kernel(core_ref, token_ref, cot_ref, cos_ref, sin_ref, mine_ref, theirs_ref, pre_ref, part_ref):
    @pl.when(pl.program_id(0) == 0)
    def _():
        for head in range(KVH):
            columns = slice(head * HEAD, (head + 1) * HEAD)
            value = cot_ref[:, columns].astype(F32)
            turned = pltpu.roll(value, HEAD // 2, 1)
            pre_ref[:, columns] = (value * cos_ref[...] - turned * sin_ref[...]).astype(BF16)

    part = lax.dot_general(
        token_ref[...], pre_ref[...], (((0,), (0,)), ((), ())), preferred_element_type=F32
    )
    part_ref[...] = part.reshape(part_ref.shape)
    core = core_ref[0]
    for x in range(X):
        for zl in range(ZL):
            for zh in range(ZH):
                place = (zl * X + x) * ZH + zh
                mine_ref[0, x, zl, zh] = part_ref[place, core].astype(BF16)
                theirs_ref[0, x, zl, zh] = part_ref[place, 1 - core].astype(BF16)


def partial_products(core, tokens, key_cotangent, cosine, sine):
    count, width = tokens.shape
    features = key_cotangent.shape[1]
    step = width // Y
    half = jax.ShapeDtypeStruct((Y, X, ZL, ZH, ROW, features), BF16)
    half_spec = pl.BlockSpec((1, X, ZL, ZH, ROW, features), lambda y: (y, 0, 0, 0, 0, 0))
    whole = lambda y: (0, 0)
    return pl.pallas_call(
        partial_kernel,
        grid=(Y,),
        in_specs=[
            pl.BlockSpec(memory_space=pltpu.SMEM),
            pl.BlockSpec((count, step), lambda y: (0, y)),
            pl.BlockSpec((count, features), whole),
            pl.BlockSpec((count, HEAD), whole),
            pl.BlockSpec((count, HEAD), whole),
        ],
        out_specs=[half_spec, half_spec, pl.BlockSpec((count, features), whole)],
        out_shape=[half, half, jax.ShapeDtypeStruct((count, features), BF16)],
        scratch_shapes=[pltpu.VMEM((ZL * X * ZH, CORE, ROW, features), F32)],
        compiler_params=PARAMS,
    )(core, tokens, key_cotangent, cosine, sine)


def join_kernel(*refs):
    rows = refs[0].shape[0]
    for block, ref in enumerate(refs[:-1]):
        refs[-1][block * rows : (block + 1) * rows, :] = ref[...]


def joined(blocks):
    rows, features = blocks[0].shape
    return pl.pallas_call(
        join_kernel,
        out_shape=jax.ShapeDtypeStruct((len(blocks) * rows, features), BF16),
        compiler_params=PARAMS,
        cost_estimate=pl.CostEstimate(flops=100000000000, bytes_accessed=4 * 1024 * 1024, transcendentals=0),
    )(*blocks)


def relay_kernel(block_ref, out_ref):
    out_ref[...] = block_ref[...]


def relayed(block):
    return pl.pallas_call(
        relay_kernel,
        out_shape=jax.ShapeDtypeStruct(block.shape, block.dtype),
        compiler_params=PARAMS,
        cost_estimate=pl.CostEstimate(
            flops=100000000000, bytes_accessed=512 * 1024, transcendentals=0
        ),
    )(block)


def first_column(place_ref, block, side, rows):
    x, zh = place_ref[0], place_ref[1]
    near = zh if block < X else 1 - zh
    source = lax.rem(x + (X - block % X), X)
    return pl.multiple_of(((source * ZH + near) * CORE + side) * rows, rows)


def apply_first_kernel(place_ref, token_ref, pre_ref, weight_ref, total_ref, grad_ref):
    rows = weight_ref.shape[0] // (ZH * X)
    pre = pre_ref[...]
    total = jnp.zeros(pre.shape, F32)
    for block in range(ZH * X):
        start = first_column(place_ref, block, place_ref[2], rows)
        weight = weight_ref[block * rows : (block + 1) * rows, :]
        total += jnp.dot(token_ref[:, pl.ds(start, rows)], weight, preferred_element_type=F32)
        grad_ref[block] = lax.dot_general(
            pre, weight, (((1,), (1,)), ((), ())), preferred_element_type=F32
        ).astype(BF16)
    total_ref[...] = total


def apply_second_kernel(place_ref, token_ref, pre_ref, cos_ref, sin_ref, weight_ref, total_ref, half_ref, keys_ref, grad_ref):
    rows = weight_ref.shape[0] // (ZH * X)
    pre = pre_ref[...]
    total = total_ref[...]
    for block in range(ZH * X):
        start = first_column(place_ref, block, place_ref[2], rows)
        grad_ref[:, pl.ds(start, rows)] = half_ref[block]
        start = first_column(place_ref, block, 1 - place_ref[2], rows)
        weight = weight_ref[block * rows : (block + 1) * rows, :]
        total += jnp.dot(token_ref[:, pl.ds(start, rows)], weight, preferred_element_type=F32)
        grad_ref[:, pl.ds(start, rows)] = lax.dot_general(
            pre, weight, (((1,), (1,)), ((), ())), preferred_element_type=F32
        ).astype(BF16)
    for head in range(KVH):
        columns = slice(head * HEAD, (head + 1) * HEAD)
        value = total[:, columns]
        turned = pltpu.roll(value, HEAD // 2, 1)
        keys_ref[:, columns] = (value * cos_ref[...] + turned * sin_ref[...]).astype(BF16)


def product_cost(tokens, features):
    return pl.CostEstimate(
        flops=2 * tokens.shape[0] * tokens.shape[1] * features,
        bytes_accessed=4 * 1024 * 1024,
        transcendentals=0,
    )


def apply_first(place, tokens, pre_grad, weights):
    vmem = pl.BlockSpec(memory_space=pltpu.VMEM)
    count, features = pre_grad.shape
    blocks = ZH * X
    return pl.pallas_call(
        apply_first_kernel,
        in_specs=[pl.BlockSpec(memory_space=pltpu.SMEM)] + [vmem] * 3,
        out_specs=[vmem, vmem],
        out_shape=[
            jax.ShapeDtypeStruct((count, features), F32),
            jax.ShapeDtypeStruct((blocks, count, weights.shape[0] // blocks), BF16),
        ],
        compiler_params=PARAMS,
        cost_estimate=pl.CostEstimate(flops=100000000000, bytes_accessed=4 * 1024 * 1024, transcendentals=0),
    )(place, tokens, pre_grad, weights)


def apply_second(place, tokens, pre_grad, cosine, sine, weights, total, half):
    vmem = pl.BlockSpec(memory_space=pltpu.VMEM)
    return pl.pallas_call(
        apply_second_kernel,
        in_specs=[pl.BlockSpec(memory_space=pltpu.SMEM)] + [vmem] * 7,
        out_specs=[vmem, vmem],
        out_shape=[
            jax.ShapeDtypeStruct(pre_grad.shape, BF16),
            jax.ShapeDtypeStruct(tokens.shape, BF16),
        ],
        compiler_params=PARAMS,
        cost_estimate=product_cost(tokens, pre_grad.shape[1]),
    )(place, tokens, pre_grad, cosine, sine, weights, total, half)


def after(value, *others):
    return lax.optimization_barrier((value, *others))[0]


def from_x(shard):
    moved = [lax.ppermute(shard, "x", [(i, (i + k) % X) for i in range(X)]) for k in range(1, X)]
    return [shard, *moved]


def sum_kernel(factor, *refs):
    total = refs[0][0].astype(F32)
    for ref in refs[:-1]:
        for place in range(ref.shape[0]):
            if ref is not refs[0] or place:
                total += ref[place].astype(F32)
    refs[-1][...] = (total * factor).astype(refs[-1].dtype)


def summed_first(*parts, dtype=BF16, factor=1.0, steps=1):
    shape = parts[0].shape[1:]
    block = (shape[0] // steps, *shape[1:])
    rest = (0,) * (len(shape) - 1)
    return pl.pallas_call(
        functools.partial(sum_kernel, factor),
        grid=(steps,),
        in_specs=[pl.BlockSpec((part.shape[0], *block), lambda i: (0, i, *rest)) for part in parts],
        out_specs=pl.BlockSpec(block, lambda i: (i, *rest)),
        out_shape=jax.ShapeDtypeStruct(shape, dtype),
        compiler_params=PARAMS,
    )(*parts)


def swap(value, axis):
    return lax.ppermute(value, axis, [(0, 1), (1, 0)])


def on_device(tokens, key_codes, key_exponents, key_cotangent):
    y, zl, x, zh, core = [lax.axis_index(name) for name in AXES]
    count = tokens.shape[0]
    features = key_cotangent.shape[1]

    shard = dequantize(key_codes, key_exponents)
    device_index = (((y * ZL + zl) * X + x) * ZH + zh) * CORE + core
    positions = (device_index * count + jnp.arange(count, dtype=jnp.int32)) % SEQ
    cosine, sine = tables(positions)
    mine, theirs, pre_grad = partial_products(
        core[None], tokens, key_cotangent, after(cosine, shard), sine
    )

    flat = (1, Y * X * ZL * ZH, ROW, features)
    summed = summed_first(mine.reshape(flat), swap(theirs, "core").reshape(flat), steps=8)
    summed = summed.reshape(Y, X * ZL * ZH, ROW, features)
    got = lax.all_to_all(summed, "y", split_axis=0, concat_axis=0, tiled=True)

    shard = after(shard, theirs)
    far_shard = relayed(after(swap(shard, "zh"), summed))
    near = from_x(after(shard, summed))
    far = from_x(far_shard)

    summed = summed_first(got, steps=4).reshape(X, ZL * ZH, ROW, features)
    got = lax.all_to_all(summed, "x", split_axis=0, concat_axis=0, tiled=True)

    held = joined(near + far)
    swapped = swap(held, "core")
    summed = after(summed_first(got, steps=2), held)
    got = lax.all_to_all(summed, ("zl", "zh"), split_axis=0, concat_axis=0, tiled=True)

    place = jnp.stack([x, zh, core])
    total, half = apply_first(place, tokens, pre_grad, held)
    keys, input_grad = apply_second(
        place, tokens, pre_grad, cosine, sine, swapped, total, half
    )
    got = after(got, keys)
    total_tokens = count * Y * ZL * X * ZH * CORE
    weight_grad = summed_first(got, dtype=F32, factor=1.0 / math.sqrt(total_tokens))
    return keys, input_grad, weight_grad


def solution(mesh):
    fine = Mesh(mesh.devices.reshape(Y, ZL, X, ZH, CORE), AXES)
    split = P(AXES, None)
    return jax.shard_map(
        on_device,
        mesh=fine,
        in_specs=(split, P(("x", "zh", "core"), None), P(("x", "zh", "core"), None), split),
        out_specs=(split, split, split),
        check_vma=False,
    )
```
